32 devices in a mesh: gx: 4 (over z), gy: 8 (over y, x, core).
Axes of the slice: x: 2, y: 2, z: 4, core: 2. Of those that a mesh axis runs over, the one named last changes fastest.
Arguments:
- psi_start: float32 [6, 131072], P(None, ('gx', 'gy')), may hold values from -6 to 6
- adjoint_rhs: float32 [6, 131072], P(None, ('gx', 'gy')), may hold values from -6 to 6
- off_blocks: bfloat16 [6, 6, 6, 131072], P(None, None, None, ('gx', 'gy')), may hold values from -0.3984375 to 0.3984375
- diag_inverse: float32 [6, 6, 131072], P(None, None, ('gx', 'gy')), may hold values from -1 to 1.5, as said below
- face_nbrs: int32 [6, 131072], P(None, ('gx', 'gy')), may hold values from 0 to 8192
- halo_lists: int32 [4, 32768], P(None, ('gx', 'gy')), may hold values from 0 to 4095
- owner_lists: int32 [4, 131072], P(None, ('gx', 'gy')), may hold values from 0 to 4096, as said below
- parent_slots: int32 [2, 64, 128, 128], P(None, 'gx', 'gy'), may hold values from 0 to 16383, as said below
- parent_weights: float32 [2, 64, 128, 128], P(None, 'gx', 'gy'), may hold values from 0.2 to 1
- fine_state: float32 [6, 64, 128, 128], P(None, 'gx', 'gy'), may hold values from -6 to 6
- fine_source: float32 [6, 64, 128, 128], P(None, 'gx', 'gy'), may hold values from -6 to 6
- coupling: float32 [6, 6], replicated, may hold values from -0.375 to 0.375
Outputs:
- psi_coarse: float32 [6, 131072], P(None, ('gx', 'gy'))
- indicator: float32 [64, 128, 128], P('gx', 'gy')
The draws below stay inside these ranges and needn't reach their ends.
Inputs may be any that keep to these rules, and one draw needn't show every extreme that they name: `owner_lists`: list k = 2 i + j of coarse partition (p, q) goes to fine partition (p - i, q - j); its live coarse cell ids fill its first slots and 4096 the rest; at most 4096 live, none where that fine partition does not exist, and one fine partition receives 4096 live from each of its four sources. `parent_slots`: each entry k * 4096 + m names a live slot m of list k received by this fine partition. `diag_inverse`: diagonal entries of each block are positive; each off-diagonal entry is at most 0.6 times its column's diagonal entry in magnitude.
All inputs are finite; a program needn't handle non-finite values.
Results may differ from the reference program's by a relative error of at most 0.0003.
Values sent between devices are 32-bit elements; how exact they have to be, the bound alone decides.
A program may use at most 128 MiB of HBM per device.

```python
import jax
import jax.numpy as jnp
from jax import lax

COMP = 6
FACES = 6
SWEEPS = 2
COARSE_DEV = 4096
HALO = 1024
CAP = 4096
FA = 16
FB = 16
FZ = 128
CELLS = 131072
NA = 64
NB = 128
N_GX = 4
N_GY = 8


def route_counts(key):
    key = jax.random.fold_in(key, 101)
    key_load, key_base, key_fa, key_fb = jax.random.split(key, 4)
    load = jax.random.randint(key_load, (N_GX, N_GY), 1, 5)
    base = jax.random.randint(key_base, (4, N_GX, N_GY), max(1, CAP // 8), max(1, CAP // 8) + max(1, CAP // 8) + 1)
    counts = jnp.minimum(CAP, base * load[None])
    shift_a = (jnp.arange(4) // 2)[:, None, None]
    shift_b = (jnp.arange(4) % 2)[:, None, None]
    along = jnp.arange(N_GX)[None, :, None]
    across = jnp.arange(N_GY)[None, None, :]
    valid = (along + shift_a < N_GX) & (across + shift_b < N_GY)
    full_a = jax.random.randint(key_fa, (), 0, N_GX - 1)
    full_b = jax.random.randint(key_fb, (), 0, N_GY - 1)
    is_full = (along == full_a) & (across == full_b)
    counts = jnp.where(is_full, CAP, counts)
    counts = jnp.where(valid, counts, 0)
    return (counts.astype(jnp.int32), full_a, full_b)


def draw_owner_lists(key, part):
    counts, full_a, full_b = route_counts(key)
    key = jax.random.fold_in(key, 7)
    shift_a = (jnp.arange(4) // 2)[:, None, None]
    shift_b = (jnp.arange(4) % 2)[:, None, None]
    which = jnp.arange(4)[:, None, None]
    along = jnp.arange(N_GX)[None, :, None] - shift_a
    across = jnp.arange(N_GY)[None, None, :] - shift_b
    exists = (along >= 0) & (across >= 0)
    source_counts = counts[which, jnp.maximum(along, 0), jnp.maximum(across, 0)]
    source_counts = jnp.where(exists, source_counts, 0)
    cells = jax.random.randint(key, (4, N_GX, N_GY, CAP), 0, COARSE_DEV)
    slot = jnp.arange(CAP)[None, None, None, :]
    lists = jnp.where(slot < source_counts[..., None], cells, COARSE_DEV)
    return lists.reshape(4, N_GX * N_GY * CAP).astype(jnp.int32)


def draw_parent_slots(key, part):
    counts, full_a, full_b = route_counts(key)
    key = jax.random.fold_in(key, 9)
    key_src, key_slot = jax.random.split(key)
    along = jnp.broadcast_to((jnp.arange(NA) // FA)[None, :, None, None], (2, NA, NB, FZ))
    across = jnp.broadcast_to((jnp.arange(NB) // FB)[None, None, :, None], (2, NA, NB, FZ))
    which = jax.random.randint(key_src, (2, NA, NB, FZ), 0, 4)
    live = counts[which, along, across]
    which = jnp.where(live > 0, which, 0)
    live = counts[which, along, across]
    slot = jax.random.randint(key_slot, (2, NA, NB, FZ), 0, 1048576) % live
    slots = (which * CAP + slot).astype(jnp.int32)
    row_a = full_a * FA
    row_b = full_b * FB
    slots = slots.at[0, row_a, row_b, 0].set(4 * CAP - 1)
    slots = slots.at[1, row_a, row_b, 0].set(0)
    return slots.astype(jnp.int32)


def draw_diag_inverse(key, part):
    key = jax.random.fold_in(key, 3)
    cells = COARSE_DEV * N_GX * N_GY
    key_diag, key_off = jax.random.split(key)
    rows = jnp.arange(COMP)[:, None, None]
    cols = jnp.arange(COMP)[None, :, None]
    unit = (rows == cols).astype(jnp.float32)
    diag = jnp.exp(jax.random.uniform(key_diag, (1, COMP, cells), jnp.float32, -0.4, 0.4))
    off = 0.2 * jnp.clip(jax.random.normal(key_off, (COMP, COMP, cells), jnp.float32), -3.0, 3.0)
    return (unit * diag + (1.0 - unit) * off * diag).astype(jnp.float32)


def set_ends(entries, stream_key, least, high):
    index_at = [jax.random.randint(jax.random.fold_in(stream_key, axis), (), 0, length) for axis, length in enumerate(entries.shape)]
    widest = entries.shape.index(max(entries.shape))
    beside = index_at[:widest] + [(index_at[widest] + 1) % entries.shape[widest]] + index_at[widest + 1:]
    return entries.at[tuple(index_at)].set(least).at[tuple(beside)].set(high)


def shard_levels(stream_key, dims, shards, least, high):
    def one(dim, blocks):
        heights = jax.random.uniform(jax.random.fold_in(jax.random.fold_in(stream_key, 6), dim), (blocks,), jnp.float32, least / len(shards), high / len(shards))
        return jnp.repeat(jnp.exp(heights), dims[dim] // blocks).reshape((-1,) + (1,) * (len(dims) - dim - 1))

    level = one(*shards[0])
    for cut in shards[1:]:
        level = level * one(*cut)
    return level


def bell_draw(own_key, shape, width, most, cuts=(), held_as=jnp.bfloat16):
    result = width * jax.random.normal(own_key, shape, jnp.float32)
    if cuts:
        result = result * shard_levels(own_key, shape, cuts, -0.22, 0.18)
    return jnp.clip(result, -most, most).astype(held_as)


def setup_inputs(seed: int = 0) -> dict:
    streams_of = jax.random.split(jax.random.key(seed), 13)
    return {
        "psi_start": bell_draw(streams_of[0], (COMP, CELLS), 1.0, 6.0, ((1, 32),), jnp.float32),
        "adjoint_rhs": bell_draw(streams_of[1], (COMP, CELLS), 1.0, 6.0, ((1, 32),), jnp.float32),
        "off_blocks": bell_draw(streams_of[2], (FACES, COMP, COMP, CELLS), 0.06, 0.3984375, ((3, 32),)),
        "diag_inverse": draw_diag_inverse(jax.random.fold_in(streams_of[12], 71), 0),
        "face_nbrs": set_ends(jax.random.randint(streams_of[4], (FACES, CELLS), 0, COARSE_DEV + 4 * HALO + 1), jax.random.fold_in(streams_of[4], 1), 0, COARSE_DEV + 4 * HALO).astype(jnp.int32),
        "halo_lists": set_ends(jax.random.randint(streams_of[5], (4, N_GX * N_GY * HALO), 0, COARSE_DEV), jax.random.fold_in(streams_of[5], 1), 0, COARSE_DEV - 1).astype(jnp.int32),
        "owner_lists": draw_owner_lists(jax.random.fold_in(streams_of[12], 71), 0),
        "parent_slots": draw_parent_slots(jax.random.fold_in(streams_of[12], 71), 0),
        "parent_weights": jnp.clip(0.2 + 0.8 * jax.random.uniform(streams_of[8], (2, NA, NB, FZ), jnp.float32) ** shard_levels(streams_of[8], (2, NA, NB, FZ), ((1, 4), (2, 8)), -0.2, 0.2), 0.2, 1.0),
        "fine_state": bell_draw(streams_of[9], (COMP, NA, NB, FZ), 1.0, 6.0, ((1, 4), (2, 8)), jnp.float32),
        "fine_source": bell_draw(streams_of[10], (COMP, NA, NB, FZ), 1.0, 6.0, ((1, 4), (2, 8)), jnp.float32),
        "coupling": bell_draw(streams_of[11], (COMP, COMP), 252 ** -0.5, 0.375, (), jnp.float32),
    }


def extend(psi, halo_lists):
    nd = N_GX * N_GY
    own = psi.reshape(COMP, N_GX, N_GY, COARSE_DEV)
    lists = halo_lists.reshape(4, N_GX, N_GY, HALO)
    packs = []
    for row in range(4):
        index = jnp.broadcast_to(lists[row][None], (COMP, N_GX, N_GY, HALO))
        packs.append(jnp.take_along_axis(own, index, axis=3))
    zero_pass = jnp.zeros((COMP, 1, N_GY, HALO), jnp.float32)
    zero_pitch = jnp.zeros((COMP, N_GX, 1, HALO), jnp.float32)
    recv_zero = jnp.concatenate([zero_pass, packs[0][:, :-1]], axis=1)
    recv_one = jnp.concatenate([packs[1][:, 1:], zero_pass], axis=1)
    recv_two = jnp.concatenate([zero_pitch, packs[2][:, :, :-1]], axis=2)
    recv_three = jnp.concatenate([packs[3][:, :, 1:], zero_pitch], axis=2)
    empty = jnp.zeros((COMP, N_GX, N_GY, 1), jnp.float32)
    whole = jnp.concatenate([own, recv_zero, recv_one, recv_two, recv_three, empty], axis=3)
    return whole.reshape(COMP, nd, COARSE_DEV + 4 * HALO + 1)


def to_parts(array, lead):
    shaped = array.reshape(lead, N_GX, FA, N_GY, FB, FZ).transpose(0, 1, 3, 2, 4, 5)
    return shaped.reshape(lead, N_GX * N_GY, FA * FB * FZ)


def reference(psi_start, adjoint_rhs, off_blocks, diag_inverse, face_nbrs, halo_lists, owner_lists, parent_slots, parent_weights, fine_state, fine_source, coupling):
    nd = N_GX * N_GY
    nbrs = face_nbrs.reshape(FACES, nd, COARSE_DEV)
    psi = psi_start
    for sweep in range(SWEEPS):
        ext = extend(psi, halo_lists)
        acc = adjoint_rhs
        for face in range(FACES):
            index = jnp.broadcast_to(nbrs[face][None], (COMP, nd, COARSE_DEV))
            values = jnp.take_along_axis(ext, index, axis=2).reshape(COMP, nd * COARSE_DEV)
            for row in range(COMP):
                acc = acc - off_blocks[face, row].astype(jnp.float32) * values[row][None]
        fresh = jnp.zeros((COMP, nd * COARSE_DEV), jnp.float32)
        for row in range(COMP):
            fresh = fresh + diag_inverse[row] * acc[row][None]
        psi = fresh
    padded = jnp.concatenate([psi.reshape(COMP, N_GX, N_GY, COARSE_DEV), jnp.zeros((COMP, N_GX, N_GY, 1), jnp.float32)], axis=3)
    lists = owner_lists.reshape(4, N_GX, N_GY, CAP)
    pieces = []
    for which in range(4):
        index = jnp.broadcast_to(lists[which][None], (COMP, N_GX, N_GY, CAP))
        sent = jnp.take_along_axis(padded, index, axis=3)
        if which // 2 == 1:
            sent = jnp.concatenate([sent[:, 1:], jnp.zeros((COMP, 1, N_GY, CAP), jnp.float32)], axis=1)
        if which % 2 == 1:
            sent = jnp.concatenate([sent[:, :, 1:], jnp.zeros((COMP, N_GX, 1, CAP), jnp.float32)], axis=2)
        pieces.append(sent)
    received = jnp.concatenate(pieces, axis=3).reshape(COMP, nd, 4 * CAP)
    slots = to_parts(parent_slots, 2)
    weights = to_parts(parent_weights, 2)
    count = FA * FB * FZ
    first = jnp.take_along_axis(received, jnp.broadcast_to(slots[0][None], (COMP, nd, count)), axis=2)
    second = jnp.take_along_axis(received, jnp.broadcast_to(slots[1][None], (COMP, nd, count)), axis=2)
    fine_psi = weights[0][None] * first + weights[1][None] * second
    fine_psi = fine_psi.reshape(COMP, N_GX, N_GY, FA, FB, FZ).transpose(0, 1, 3, 2, 4, 5).reshape(COMP, NA, NB, FZ)
    padfine = jnp.pad(fine_state, ((0, 0), (1, 1), (1, 1), (1, 1)))
    beside = padfine[:, 2:, 1:-1, 1:-1] + padfine[:, :-2, 1:-1, 1:-1]
    beside = beside + padfine[:, 1:-1, 2:, 1:-1] + padfine[:, 1:-1, :-2, 1:-1]
    beside = beside + padfine[:, 1:-1, 1:-1, 2:] + padfine[:, 1:-1, 1:-1, :-2]
    lap = 6.0 * fine_state - beside
    fine_residual = jnp.einsum("ck,kabz->cabz", coupling, lap, precision=lax.Precision.HIGHEST) + fine_source
    indicator = jnp.sum(fine_psi * fine_residual, axis=0)
    return psi, indicator
```

```python
import functools

import jax
import jax.numpy as jnp
from jax import lax
from jax.experimental import pallas as pl
from jax.experimental.pallas import tpu as pltpu
from jax.sharding import PartitionSpec as P

SWEEPS = 2
LANES = 128
MESH = pl.DeviceIdType.MESH


def lane_take(table, lanes):
    return jnp.take_along_axis(table, lanes, axis=1, mode="promise_in_bounds")


def to_rows(src, dst):
    lists, cells = src.shape
    for k in range(lists):
        for j in range(cells // LANES):
            dst[k, j : j + 1, :] = src[k : k + 1, j * LANES : (j + 1) * LANES]


def pick(indices, totals, segments, comps, unroll=8):
    lanes = [index & (LANES - 1) for index in indices]
    rows = [index >> 7 for index in indices]
    for first, count, load in segments:

        def step(j, totals):
            values = [jnp.broadcast_to(load(c, j), (8, LANES)) for c in range(comps)]
            out = []
            for u in range(len(indices)):
                here = rows[u] == first + j
                for c in range(comps):
                    out.append(jnp.where(here, lane_take(values[c], lanes[u]), totals[u * comps + c]))
            return tuple(out)

        totals = lax.fori_loop(0, count, step, tuple(totals), unroll=min(unroll, count))
    return totals


def zeros_8(count):
    return [jnp.zeros((8, LANES), jnp.float32) for _ in range(count)]


def kernel(
    peers,
    psi_start,
    rhs,
    off,
    diag,
    nbrs,
    halos,
    owners,
    slots,
    weights,
    fine,
    source,
    coupling,
    psi_out,
    indicator,
    psi_mid,
    nbr_rows,
    halo_rows,
    owner_rows,
    picked,
    halo_out,
    halo_in,
    owner_out,
    owner_in,
    grown,
    side_out,
    side_in,
    residual,
    send_sem,
    recv_sem,
):
    comps, cells = psi_start.shape
    faces = off.shape[0]
    blocks = cells // LANES
    halo_blocks = halo_rows.shape[1]
    _, fa, fb, _ = fine.shape
    n_x, n_y = peers
    p, q = lax.axis_index("gx"), lax.axis_index("gy")

    def exists(dx, dy):
        ok = None
        for pos, by, n in ((p, dx, n_x), (q, dy, n_y)):
            if by:
                one = (pos + by >= 0) & (pos + by < n)
                ok = one if ok is None else ok & one
        return ok

    halo_in[...] = jnp.zeros_like(halo_in)
    owner_in[...] = jnp.zeros_like(owner_in)
    side_in[...] = jnp.zeros_like(side_in)
    grown[:, 0:1, :, :] = jnp.zeros((comps, 1, fb + 16, LANES), jnp.float32)
    grown[:, fa + 1 : fa + 2, :, :] = jnp.zeros((comps, 1, fb + 16, LANES), jnp.float32)

    around = ((1, 0), (-1, 0), (0, 1), (0, -1))
    barrier = pltpu.get_barrier_semaphore()
    for dx, dy in around + ((-1, -1), (1, 1)):
        @pl.when(exists(dx, dy))
        def _():
            pl.semaphore_signal(barrier, inc=1, device_id=(p + dx, q + dy), device_id_type=MESH)
    side_out[0] = fine[:, :, 0, :]
    side_out[1] = fine[:, :, fb - 1, :]
    met = [jnp.where(exists(dx, dy), 1, 0) for dx, dy in around + ((-1, -1), (1, 1))]
    pl.semaphore_wait(barrier, sum(met[1:], met[0]))

    def remote(src, dst, number, dx, dy):
        return (
            pltpu.make_async_remote_copy(
                src_ref=src,
                dst_ref=dst,
                send_sem=send_sem.at[number],
                recv_sem=recv_sem.at[number],
                device_id=(p + dx, q + dy),
                device_id_type=MESH,
            ),
            dx,
            dy,
        )

    def start(copies):
        for copy, dx, dy in copies:
            @pl.when(exists(dx, dy))
            def _():
                copy.start()

    def arrive(copies):
        for copy, dx, dy in copies:
            @pl.when(exists(-dx, -dy))
            def _():
                copy.wait_recv()

    def leave(copies):
        for copy, dx, dy in copies:
            @pl.when(exists(dx, dy))
            def _():
                copy.wait_send()

    fine_copies = [
        remote(fine.at[:, fa - 1], grown.at[:, 0, 8 : 8 + fb, :], 8, 1, 0),
        remote(fine.at[:, 0], grown.at[:, fa + 1, 8 : 8 + fb, :], 9, -1, 0),
        remote(side_out.at[1], side_in.at[0], 10, 0, 1),
        remote(side_out.at[0], side_in.at[1], 11, 0, -1),
    ]
    start(fine_copies)

    to_rows(halos, halo_rows)

    def own(ref):
        return lambda c, j: ref[c : c + 1, pl.ds(pl.multiple_of(j * LANES, LANES), LANES)]

    every = []
    for sweep in range(SWEEPS):
        psi = psi_start if sweep == 0 else psi_mid
        fresh = psi_mid if sweep == 0 else psi_out
        for d in range(4):
            sums = pick([halo_rows[d]], zeros_8(comps), [(0, blocks, own(psi))], comps)
            for c in range(comps):
                halo_out[sweep, d, c] = sums[c]
        copies = [
            remote(halo_out.at[sweep, d], halo_in.at[sweep, d], sweep * 4 + d, *around[d])
            for d in range(4)
        ]
        start(copies)
        every.append(copies)
        if sweep == 0:
            to_rows(nbrs, nbr_rows)
            to_rows(owners, owner_rows)
        parts = blocks // 8
        per = 4

        def indices_of(f):
            return [nbr_rows[f, 8 * u : 8 * u + 8, :] for u in range(per)]

        @pl.loop(0, faces)
        def _(f):
            sums = pick(indices_of(f), zeros_8(per * comps), [(0, blocks, own(psi))], comps)
            for u in range(per):
                for c in range(comps):
                    picked[f, c, 8 * u : 8 * u + 8, :] = sums[u * comps + c]

        arrive(copies)

        def far(d):
            return lambda c, j: halo_in[sweep, d, c, pl.ds(j, 1), :]

        @pl.loop(0, faces)
        def _(f):
            before = [picked[f, c, 8 * u : 8 * u + 8, :] for u in range(per) for c in range(comps)]
            segments = [(blocks + halo_blocks * d, halo_blocks, far(d)) for d in range(4)]
            sums = pick(indices_of(f), before, segments, comps)
            for u in range(per):
                for c in range(comps):
                    picked[f, c, 8 * u : 8 * u + 8, :] = sums[u * comps + c]

        @pl.loop(0, blocks)
        def _(b):
            here = pl.ds(pl.multiple_of(b * LANES, LANES), LANES)
            acc = rhs[:, here]
            for f in range(faces):
                total = None
                for r in range(comps):
                    value = jnp.broadcast_to(picked[f, r, pl.ds(b, 1), :], (comps, LANES))
                    term = off[f, r, :, here].astype(jnp.float32) * value
                    total = term if total is None else total + term
                acc = acc - total
            new = None
            for r in range(comps):
                term = diag[r, :, here] * jnp.broadcast_to(acc[r : r + 1, :], (comps, LANES))
                new = term if new is None else new + term
            fresh[:, here] = new

    for k in (3, 2, 1, 0):
        lists = [owner_rows[k, 8 * u : 8 * u + 8, :] for u in range(per)]
        sums = pick(lists, zeros_8(per * comps), [(0, blocks, own(psi_out))], comps)
        target = owner_in.at[0] if k == 0 else owner_out.at[k - 1]
        for u in range(per):
            for c in range(comps):
                target[c, 8 * u : 8 * u + 8, :] = sums[u * comps + c]
        if k:
            copies = [remote(owner_out.at[k - 1], owner_in.at[k], 11 + k, -(k // 2), -(k % 2))]
            start(copies)
            every.append(copies)

    arrive(fine_copies)
    for c in range(comps):
        for a in range(fa):
            grown[c, a + 1, 8 : 8 + fb, :] = fine[c, a]
            grown[c, a + 1, 7:8, :] = side_in[0, c, a : a + 1, :]
            grown[c, a + 1, 8 + fb : 9 + fb, :] = side_in[1, c, a : a + 1, :]
    lane = lax.broadcasted_iota(jnp.int32, (8, LANES), 1)

    @pl.loop(0, fa)
    def _(a):
        for h in range(fb // 8):
            low = 8 + 8 * h
            laps = []
            for c in range(comps):
                mid = grown[c, a + 1, low : low + 8, :]
                beside = grown[c, a + 2, low : low + 8, :] + grown[c, a, low : low + 8, :]
                beside = beside + grown[c, a + 1, low + 1 : low + 9, :] + grown[c, a + 1, low - 1 : low + 7, :]
                beside = beside + jnp.where(lane == LANES - 1, 0.0, pltpu.roll(mid, LANES - 1, 1))
                beside = beside + jnp.where(lane == 0, 0.0, pltpu.roll(mid, 1, 1))
                laps.append(6.0 * mid - beside)
            for c in range(comps):
                total = source[c, a, 8 * h : 8 * h + 8, :]
                for k in range(comps):
                    total = total + coupling[c, k] * laps[k]
                residual[c, a, 8 * h : 8 * h + 8, :] = total

    for copies in every[SWEEPS:]:
        arrive(copies)

    halves = fb // 8

    @pl.loop(0, fa)
    def _(a):
        places = [(s, h) for s in range(2) for h in range(halves)]
        indices = [slots[s, a, 8 * h : 8 * h + 8, :] for s, h in places]

        def sent(k):
            return lambda c, j: owner_in[k, c, pl.ds(j, 1), :]

        segments = [(blocks * k, blocks, sent(k)) for k in range(4)]
        sums = pick(indices, zeros_8(len(places) * comps), segments, comps)
        for h in range(halves):
            here = slice(8 * h, 8 * h + 8)
            total = None
            for c in range(comps):
                value = weights[0, a, here, :] * sums[h * comps + c]
                value = value + weights[1, a, here, :] * sums[(halves + h) * comps + c]
                term = value * residual[c, a, here, :]
                total = term if total is None else total + term
            indicator[a, here, :] = total

    leave(fine_copies)
    for copies in every:
        leave(copies)


def on_device(peers, psi_start, rhs, off, diag, nbrs, halos, owners, slots, weights, fine, source, coupling):
    comps, cells = psi_start.shape
    faces = off.shape[0]
    blocks = cells // LANES
    halo_blocks = halos.shape[1] // LANES
    _, fa, fb, fz = fine.shape
    vmem = pl.BlockSpec(memory_space=pltpu.VMEM)
    return tuple(
        pl.pallas_call(
            functools.partial(kernel, peers),
            out_shape=(
                jax.ShapeDtypeStruct((comps, cells), jnp.float32),
                jax.ShapeDtypeStruct((fa, fb, fz), jnp.float32),
            ),
            in_specs=[vmem] * 11 + [pl.BlockSpec(memory_space=pltpu.SMEM)],
            out_specs=(vmem, vmem),
            scratch_shapes=[
                pltpu.VMEM((comps, cells), jnp.float32),
                pltpu.VMEM((faces, blocks, LANES), jnp.int32),
                pltpu.VMEM((4, halo_blocks, LANES), jnp.int32),
                pltpu.VMEM((4, blocks, LANES), jnp.int32),
                pltpu.VMEM((faces, comps, blocks, LANES), jnp.float32),
                pltpu.VMEM((SWEEPS, 4, comps, halo_blocks, LANES), jnp.float32),
                pltpu.VMEM((SWEEPS, 4, comps, halo_blocks, LANES), jnp.float32),
                pltpu.VMEM((3, comps, blocks, LANES), jnp.float32),
                pltpu.VMEM((4, comps, blocks, LANES), jnp.float32),
                pltpu.VMEM((comps, fa + 2, fb + 16, LANES), jnp.float32),
                pltpu.VMEM((2, comps, fa, LANES), jnp.float32),
                pltpu.VMEM((2, comps, fa, LANES), jnp.float32),
                pltpu.VMEM((comps, fa, fb, LANES), jnp.float32),
                pltpu.SemaphoreType.DMA((15,)),
                pltpu.SemaphoreType.DMA((15,)),
            ],
            compiler_params=pltpu.CompilerParams(
                collective_id=0, has_side_effects=True, vmem_limit_bytes=40 * 2**20
            ),
            name="indicators",
        )(psi_start, rhs, off, diag, nbrs, halos, owners, slots, weights, fine, source, coupling)
    )


def solution(mesh):
    placed = (
        P(None, ("gx", "gy")),
        P(None, ("gx", "gy")),
        P(None, None, None, ("gx", "gy")),
        P(None, None, ("gx", "gy")),
        P(None, ("gx", "gy")),
        P(None, ("gx", "gy")),
        P(None, ("gx", "gy")),
        P(None, "gx", "gy", None),
        P(None, "gx", "gy", None),
        P(None, "gx", "gy", None),
        P(None, "gx", "gy", None),
        P(),
    )
    return jax.shard_map(
        functools.partial(on_device, (mesh.shape["gx"], mesh.shape["gy"])),
        mesh=mesh,
        in_specs=placed,
        out_specs=(P(None, ("gx", "gy")), P("gx", "gy", None)),
        check_vma=False,
    )
```

```python
import functools

import jax
import jax.numpy as jnp
from jax import lax
from jax.experimental import pallas as pl
from jax.experimental.pallas import tpu as pltpu
from jax.sharding import PartitionSpec as P

SWEEPS = 2
LANES = 128
LEVELS = 32767.0
MESH = pl.DeviceIdType.MESH


def lane_take(table, lanes):
    return jnp.take_along_axis(table, lanes, axis=1, mode="promise_in_bounds")


def to_rows(src, dst):
    lists, cells = src.shape
    for k in range(lists):
        for j in range(cells // LANES):
            dst[k, j : j + 1, :] = src[k : k + 1, j * LANES : (j + 1) * LANES]


def pick(indices, totals, segments, comps):
    totals = list(totals)
    for u, index in enumerate(indices):
        lanes, rows = index & (LANES - 1), index >> 7
        for first, count, load in segments:
            for j in range(count):
                here = rows == first + j
                for c in range(comps):
                    value = jnp.broadcast_to(load(c, j), (8, LANES))
                    at = u * comps + c
                    totals[at] = jnp.where(here, lane_take(value, lanes), totals[at])
    return totals


def zeros_8(count, dtype=jnp.float32):
    return [jnp.zeros((8, LANES), dtype) for _ in range(count)]


def peak_of(values):
    return jnp.maximum(jnp.max(jnp.abs(values)), 1e-30)


def coded(value, scale):
    root = jnp.sqrt(jnp.sqrt(jnp.abs(value) * scale)) * LEVELS + 0.5
    return jnp.where(value < 0.0, -root, root).astype(jnp.int32)


def pair_coded(first, second, peak):
    scale = 1.0 / peak
    return coded(first, scale) * 65536 + coded(second, scale)


def decoded(code, peak):
    root = code.astype(jnp.float32) * (1.0 / LEVELS)
    square = root * root
    value = square * square * peak
    return jnp.where(code < 0, -value, value)


def pair_decoded(word, peak):
    first = (word + 32768) >> 16
    return decoded(first, peak), decoded(word - first * 65536, peak)


def kernel(
    peers,
    psi_start,
    rhs,
    off,
    diag,
    nbrs,
    halos,
    owners,
    slots,
    weights,
    fine,
    source,
    coupling,
    psi_out,
    indicator,
    psi_mid,
    nbr_rows,
    halo_rows,
    owner_rows,
    picked,
    halo_out,
    halo_in,
    owner_out,
    owner_in,
    grown,
    side_out,
    side_in,
    residual,
    own_words,
    far_words,
    parent_words,
    send_sem,
    recv_sem,
):
    comps, cells = psi_start.shape
    pairs = comps // 2
    faces = off.shape[0]
    blocks = cells // LANES
    halo_blocks = halo_rows.shape[1]
    _, fa, fb, _ = fine.shape
    n_x, n_y = peers
    p, q = lax.axis_index("gx"), lax.axis_index("gy")

    def exists(dx, dy):
        ok = None
        for pos, by, n in ((p, dx, n_x), (q, dy, n_y)):
            if by:
                one = (pos + by >= 0) & (pos + by < n)
                ok = one if ok is None else ok & one
        return ok

    halo_in[...] = jnp.zeros_like(halo_in)
    owner_in[...] = jnp.zeros_like(owner_in)
    side_in[...] = jnp.zeros_like(side_in)
    grown[:, 0:1, :, :] = jnp.zeros((comps, 1, fb + 16, LANES), jnp.float32)
    grown[:, fa + 1 : fa + 2, :, :] = jnp.zeros((comps, 1, fb + 16, LANES), jnp.float32)

    around = ((1, 0), (-1, 0), (0, 1), (0, -1))
    barrier = pltpu.get_barrier_semaphore()
    for dx, dy in around + ((-1, -1), (1, 1)):
        @pl.when(exists(dx, dy))
        def _():
            pl.semaphore_signal(barrier, inc=1, device_id=(p + dx, q + dy), device_id_type=MESH)
    side_out[0] = fine[:, :, 0, :]
    side_out[1] = fine[:, :, fb - 1, :]
    met = [jnp.where(exists(dx, dy), 1, 0) for dx, dy in around + ((-1, -1), (1, 1))]
    pl.semaphore_wait(barrier, sum(met[1:], met[0]))

    def remote(src, dst, number, dx, dy):
        return (
            pltpu.make_async_remote_copy(
                src_ref=src,
                dst_ref=dst,
                send_sem=send_sem.at[number],
                recv_sem=recv_sem.at[number],
                device_id=(p + dx, q + dy),
                device_id_type=MESH,
            ),
            dx,
            dy,
        )

    def start(copies):
        for copy, dx, dy in copies:
            @pl.when(exists(dx, dy))
            def _():
                copy.start()

    def arrive(copies):
        for copy, dx, dy in copies:
            @pl.when(exists(-dx, -dy))
            def _():
                copy.wait_recv()

    def leave(copies):
        for copy, dx, dy in copies:
            @pl.when(exists(dx, dy))
            def _():
                copy.wait_send()

    fine_copies = [
        remote(fine.at[:, fa - 1], grown.at[:, 0, 8 : 8 + fb, :], 8, 1, 0),
        remote(fine.at[:, 0], grown.at[:, fa + 1, 8 : 8 + fb, :], 9, -1, 0),
        remote(side_out.at[1], side_in.at[0], 10, 0, 1),
        remote(side_out.at[0], side_in.at[1], 11, 0, -1),
    ]
    start(fine_copies)

    to_rows(halos, halo_rows)

    def own(ref):
        return lambda c, j: ref[c : c + 1, j * LANES : (j + 1) * LANES]

    every = []
    for sweep in range(SWEEPS):
        psi = psi_start if sweep == 0 else psi_mid
        fresh = psi_mid if sweep == 0 else psi_out
        for d in range(4):
            sums = pick([halo_rows[d]], zeros_8(comps), [(0, blocks, own(psi))], comps)
            for c in range(comps):
                halo_out[sweep, d, c] = sums[c]
        copies = [
            remote(halo_out.at[sweep, d], halo_in.at[sweep, d], sweep * 4 + d, *around[d])
            for d in range(4)
        ]
        start(copies)
        every.append(copies)
        if sweep == 0:
            to_rows(nbrs, nbr_rows)
            to_rows(owners, owner_rows)
        parts = blocks // 8
        per = 4

        def indices_of(f):
            return [nbr_rows[f, 8 * u : 8 * u + 8, :] for u in range(per)]

        peak = peak_of(psi[...])
        own_words[...] = pair_coded(psi[0:pairs, :], psi[pairs:comps, :], peak)

        @pl.loop(0, faces)
        def _(f):
            sums = pick(indices_of(f), zeros_8(per * pairs, jnp.int32), [(0, blocks, own(own_words))], pairs)
            for u in range(per):
                for c in range(pairs):
                    first, second = pair_decoded(sums[u * pairs + c], peak)
                    picked[f, c, 8 * u : 8 * u + 8, :] = first
                    picked[f, c + pairs, 8 * u : 8 * u + 8, :] = second

        arrive(copies)
        far_peak = peak_of(halo_in[sweep])
        far_words[...] = pair_coded(halo_in[sweep, :, 0:pairs], halo_in[sweep, :, pairs:comps], far_peak)

        def far(d):
            return lambda c, j: far_words[d, c, j : j + 1, :]

        @pl.loop(0, faces)
        def _(f):
            segments = [(blocks + halo_blocks * d, halo_blocks, far(d)) for d in range(4)]
            sums = pick(indices_of(f), zeros_8(per * pairs, jnp.int32), segments, pairs)
            for u in range(per):
                rows = slice(8 * u, 8 * u + 8)
                for c in range(pairs):
                    first, second = pair_decoded(sums[u * pairs + c], far_peak)
                    picked[f, c, rows, :] = picked[f, c, rows, :] + first
                    picked[f, c + pairs, rows, :] = picked[f, c + pairs, rows, :] + second

        @pl.loop(0, blocks)
        def _(b):
            here = pl.ds(pl.multiple_of(b * LANES, LANES), LANES)
            acc = rhs[:, here]
            for f in range(faces):
                total = None
                for r in range(comps):
                    value = jnp.broadcast_to(picked[f, r, pl.ds(b, 1), :], (comps, LANES))
                    term = off[f, r, :, here].astype(jnp.float32) * value
                    total = term if total is None else total + term
                acc = acc - total
            new = None
            for r in range(comps):
                term = diag[r, :, here] * jnp.broadcast_to(acc[r : r + 1, :], (comps, LANES))
                new = term if new is None else new + term
            fresh[:, here] = new

    for k in (3, 2, 1, 0):
        lists = [owner_rows[k, 8 * u : 8 * u + 8, :] for u in range(per)]
        sums = pick(lists, zeros_8(per * comps), [(0, blocks, own(psi_out))], comps)
        target = owner_in.at[0] if k == 0 else owner_out.at[k - 1]
        for u in range(per):
            for c in range(comps):
                target[c, 8 * u : 8 * u + 8, :] = sums[u * comps + c]
        if k:
            copies = [remote(owner_out.at[k - 1], owner_in.at[k], 11 + k, -(k // 2), -(k % 2))]
            start(copies)
            every.append(copies)

    arrive(fine_copies)
    for c in range(comps):
        for a in range(fa):
            grown[c, a + 1, 8 : 8 + fb, :] = fine[c, a]
            grown[c, a + 1, 7:8, :] = side_in[0, c, a : a + 1, :]
            grown[c, a + 1, 8 + fb : 9 + fb, :] = side_in[1, c, a : a + 1, :]
    lane = lax.broadcasted_iota(jnp.int32, (8, LANES), 1)

    @pl.loop(0, fa)
    def _(a):
        for h in range(fb // 8):
            low = 8 + 8 * h
            laps = []
            for c in range(comps):
                mid = grown[c, a + 1, low : low + 8, :]
                beside = grown[c, a + 2, low : low + 8, :] + grown[c, a, low : low + 8, :]
                beside = beside + grown[c, a + 1, low + 1 : low + 9, :] + grown[c, a + 1, low - 1 : low + 7, :]
                beside = beside + jnp.where(lane == LANES - 1, 0.0, pltpu.roll(mid, LANES - 1, 1))
                beside = beside + jnp.where(lane == 0, 0.0, pltpu.roll(mid, 1, 1))
                laps.append(6.0 * mid - beside)
            for c in range(comps):
                total = source[c, a, 8 * h : 8 * h + 8, :]
                for k in range(comps):
                    total = total + coupling[c, k] * laps[k]
                residual[c, a, 8 * h : 8 * h + 8, :] = total

    for copies in every[SWEEPS:]:
        arrive(copies)

    halves = fb // 8
    parent_peak = peak_of(owner_in[...])

    @pl.loop(0, 4)
    def _(k):
        parent_words[k] = pair_coded(owner_in[k, 0:pairs], owner_in[k, pairs:comps], parent_peak)

    @pl.loop(0, fa)
    def _(a):
        places = [(s, h) for s in range(2) for h in range(halves)]
        indices = [slots[s, a, 8 * h : 8 * h + 8, :] for s, h in places]

        def sent(k, sums):
            return tuple(pick(indices, sums, [(blocks * k, blocks, lambda c, j: parent_words[k, c, j : j + 1, :])], pairs))

        words = lax.fori_loop(0, 4, sent, tuple(zeros_8(len(places) * pairs, jnp.int32)))
        sums = [None] * (len(places) * comps)
        for u in range(len(places)):
            for c in range(pairs):
                sums[u * comps + c], sums[u * comps + c + pairs] = pair_decoded(words[u * pairs + c], parent_peak)
        for h in range(halves):
            here = slice(8 * h, 8 * h + 8)
            total = None
            for c in range(comps):
                value = weights[0, a, here, :] * sums[h * comps + c]
                value = value + weights[1, a, here, :] * sums[(halves + h) * comps + c]
                term = value * residual[c, a, here, :]
                total = term if total is None else total + term
            indicator[a, here, :] = total

    leave(fine_copies)
    for copies in every:
        leave(copies)


def on_device(peers, psi_start, rhs, off, diag, nbrs, halos, owners, slots, weights, fine, source, coupling):
    comps, cells = psi_start.shape
    faces = off.shape[0]
    blocks = cells // LANES
    halo_blocks = halos.shape[1] // LANES
    _, fa, fb, fz = fine.shape
    vmem = pl.BlockSpec(memory_space=pltpu.VMEM)
    return tuple(
        pl.pallas_call(
            functools.partial(kernel, peers),
            out_shape=(
                jax.ShapeDtypeStruct((comps, cells), jnp.float32),
                jax.ShapeDtypeStruct((fa, fb, fz), jnp.float32),
            ),
            in_specs=[vmem] * 11 + [pl.BlockSpec(memory_space=pltpu.SMEM)],
            out_specs=(vmem, vmem),
            scratch_shapes=[
                pltpu.VMEM((comps, cells), jnp.float32),
                pltpu.VMEM((faces, blocks, LANES), jnp.int32),
                pltpu.VMEM((4, halo_blocks, LANES), jnp.int32),
                pltpu.VMEM((4, blocks, LANES), jnp.int32),
                pltpu.VMEM((faces, comps, blocks, LANES), jnp.float32),
                pltpu.VMEM((SWEEPS, 4, comps, halo_blocks, LANES), jnp.float32),
                pltpu.VMEM((SWEEPS, 4, comps, halo_blocks, LANES), jnp.float32),
                pltpu.VMEM((3, comps, blocks, LANES), jnp.float32),
                pltpu.VMEM((4, comps, blocks, LANES), jnp.float32),
                pltpu.VMEM((comps, fa + 2, fb + 16, LANES), jnp.float32),
                pltpu.VMEM((2, comps, fa, LANES), jnp.float32),
                pltpu.VMEM((2, comps, fa, LANES), jnp.float32),
                pltpu.VMEM((comps, fa, fb, LANES), jnp.float32),
                pltpu.VMEM((comps // 2, cells), jnp.int32),
                pltpu.VMEM((4, comps // 2, halo_blocks, LANES), jnp.int32),
                pltpu.VMEM((4, comps // 2, blocks, LANES), jnp.int32),
                pltpu.SemaphoreType.DMA((15,)),
                pltpu.SemaphoreType.DMA((15,)),
            ],
            compiler_params=pltpu.CompilerParams(
                collective_id=0, has_side_effects=True, vmem_limit_bytes=40 * 2**20
            ),
            name="indicators",
        )(psi_start, rhs, off, diag, nbrs, halos, owners, slots, weights, fine, source, coupling)
    )


def solution(mesh):
    placed = (
        P(None, ("gx", "gy")),
        P(None, ("gx", "gy")),
        P(None, None, None, ("gx", "gy")),
        P(None, None, ("gx", "gy")),
        P(None, ("gx", "gy")),
        P(None, ("gx", "gy")),
        P(None, ("gx", "gy")),
        P(None, "gx", "gy", None),
        P(None, "gx", "gy", None),
        P(None, "gx", "gy", None),
        P(None, "gx", "gy", None),
        P(),
    )
    return jax.shard_map(
        functools.partial(on_device, (mesh.shape["gx"], mesh.shape["gy"])),
        mesh=mesh,
        in_specs=placed,
        out_specs=(P(None, ("gx", "gy")), P("gx", "gy", None)),
        check_vma=False,
    )
```
